32 devices in a mesh: dom: 8 (over z, core), sub: 4 (over y, x).
Axes of the slice: x: 2, y: 2, z: 4, core: 2. Of those that a mesh axis runs over, the one named last changes fastest.
Arguments:
- state: float32 [9, 10, 8192], P(None, None, ('dom', 'sub')), may hold values from -6 to 6
- geometry: float32 [3, 3, 8192], P(None, None, ('dom', 'sub')), may hold values from -4 to 4
- face_scale: float32 [4, 8192], P(None, ('dom', 'sub')), may hold values from 0.2 to 1
- material: int32 [8192], P(('dom', 'sub')), may hold values from 0 to 2
- cluster: int32 [8192], P(('dom', 'sub')), may hold values from 0 to 1, as said below
- neighbours: int32 [4, 8192], P(None, ('dom', 'sub')), may hold values from 0 to 767, as said below
- orientation: int32 [4, 8192], P(None, ('dom', 'sub')), may hold values from 0 to 11
- stiffness: float32 [3, 10, 10], replicated, may hold values from -2 to 2
- jacobians: float32 [3, 3, 9, 9], replicated, may hold values from -2 to 2
- flux_local: float32 [4, 10, 10], replicated, may hold values from -2 to 2
- flux_neigh: float32 [12, 10, 10], replicated, may hold values from -2 to 2
- flux_plus: float32 [3, 9, 9], replicated, may hold values from -2 to 2
- flux_minus: float32 [3, 9, 9], replicated, may hold values from -2 to 2
Outputs:
- final_state: float32 [9, 10, 8192], P(None, None, ('dom', 'sub'))
The draws below stay inside these ranges and needn't reach their ends.
Inputs may be any that keep to these rules, and one draw needn't show every extreme that they name: Face neighbours are numbered in the table of the face's own partition, as the first step says. `cluster`: 0 marks a fine tetrahedron, 1 a coarse one.
All inputs are finite; a program needn't handle non-finite values.
Results may differ from the reference program's by a relative error of at most 0.0003.
Values sent between devices are 32-bit elements; how exact they have to be, the bound alone decides.
A program may use at most 64 MiB of HBM per device.

```python
import math
import jax
import jax.numpy as jnp
from jax import lax

QUANT = 9
BASIS = 10
ELEM_DEV = 256
COPY_DEV = 128
SUB_COPY = 64
MACRO = 1
ELEMENTS = 8192
N_DOM = 8
N_SUB = 4


def draw_cluster(key, part):
    first_key = jax.random.fold_in(key, 11)
    second_key = jax.random.fold_in(key, 12)
    percent = jax.random.randint(first_key, (N_DOM * N_SUB,), 10, 91)
    rolled = jax.random.randint(second_key, (ELEMENTS,), 0, 100)
    owner = jnp.arange(ELEMENTS, dtype=jnp.int32) // ELEM_DEV
    return jnp.where(rolled < percent[owner], 0, 1).astype(jnp.int32)


def draw_neighbours(key, part):
    local_key = jax.random.fold_in(key, 21)
    sub_key = jax.random.fold_in(key, 22)
    side_key = jax.random.fold_in(key, 23)
    local_pick = jax.random.randint(local_key, (4, ELEMENTS), 0, ELEM_DEV)
    sub_pick = jax.random.randint(sub_key, (ELEMENTS,), 0, N_SUB * SUB_COPY)
    side_pick = jax.random.randint(side_key, (2, ELEMENTS), 0, COPY_DEV)
    local = jnp.arange(ELEMENTS, dtype=jnp.int32) % ELEM_DEV
    left_start = ELEM_DEV + N_SUB * SUB_COPY
    right_start = left_start + COPY_DEV
    face_zero = jnp.where(local < SUB_COPY, ELEM_DEV + sub_pick, local_pick[0])
    face_one = jnp.where(local >= ELEM_DEV - COPY_DEV, right_start + side_pick[0], local_pick[1])
    face_two = jnp.where(local < COPY_DEV, left_start + side_pick[1], local_pick[2])
    return jnp.stack([face_zero, face_one, face_two, local_pick[3]]).astype(jnp.int32)


def place_ends(values, key, smallest, top_value):
    place = [jax.random.randint(jax.random.fold_in(key, axis), (), 0, length) for axis, length in enumerate(values.shape)]
    longest = values.shape.index(max(values.shape))
    neighbour = place[:longest] + [(place[longest] + 1) % values.shape[longest]] + place[longest + 1:]
    return values.at[tuple(place)].set(smallest).at[tuple(neighbour)].set(top_value)


def steps_of(stream_key, extent, cuts, least, top_value):
    gain, own = 1.0, jax.random.fold_in(stream_key, 6)
    for dim, blocks in cuts:
        heights = jnp.exp(jax.random.uniform(jax.random.fold_in(own, dim), (blocks,), jnp.float32, least / len(cuts), top_value / len(cuts)))
        gain = gain * jnp.repeat(heights, extent[dim] // blocks).reshape([-1 if axis == dim else 1 for axis in range(len(extent))])
    return gain


def bell_draw(rng, dims, width, reach, shards=(), held_as=jnp.bfloat16):
    entries = width * jax.random.normal(rng, dims, jnp.float32)
    if shards:
        entries = entries * steps_of(rng, dims, shards, -0.22, 0.18)
    return jnp.clip(entries, -reach, reach).astype(held_as)


def setup_inputs(seed: int = 0) -> dict:
    seeds = jax.random.split(jax.random.key(seed), 14)
    state = bell_draw(seeds[0], (QUANT, BASIS, ELEMENTS), 1.0, 6.0, ((2, 32),), jnp.float32)
    geometry = bell_draw(seeds[1], (3, 3, ELEMENTS), 0.6, 4.0, ((2, 32),), jnp.float32)
    face_scale = jnp.clip(jnp.exp(math.log(1.0) - 1.609438 * jax.random.uniform(seeds[2], (4, ELEMENTS), jnp.float32) ** steps_of(seeds[2], (4, ELEMENTS), ((1, 32),), -0.2, 0.2)), 0.2, 1.0)
    material = place_ends(jax.random.randint(seeds[3], (ELEMENTS,), 0, 3), jax.random.fold_in(seeds[3], 1), 0, 2).astype(jnp.int32)
    cluster = draw_cluster(jax.random.fold_in(seeds[13], 71), 0)
    neighbours = draw_neighbours(jax.random.fold_in(seeds[13], 71), 0)
    orientation = place_ends(jax.random.randint(seeds[6], (4, ELEMENTS), 0, 12), jax.random.fold_in(seeds[6], 1), 0, 11).astype(jnp.int32)
    stiffness = bell_draw(seeds[7], (3, BASIS, BASIS), BASIS ** -0.5, 2.0, (), jnp.float32)
    jacobians = bell_draw(seeds[8], (3, 3, QUANT, QUANT), QUANT ** -0.5, 2.0, (), jnp.float32)
    flux_local = bell_draw(seeds[9], (4, BASIS, BASIS), BASIS ** -0.5, 2.0, (), jnp.float32)
    flux_neigh = bell_draw(seeds[10], (12, BASIS, BASIS), BASIS ** -0.5, 2.0, (), jnp.float32)
    flux_plus = bell_draw(seeds[11], (3, QUANT, QUANT), QUANT ** -0.5, 2.0, (), jnp.float32)
    flux_minus = bell_draw(seeds[12], (3, QUANT, QUANT), QUANT ** -0.5, 2.0, (), jnp.float32)
    return {"state": state, "geometry": geometry, "face_scale": face_scale, "material": material, "cluster": cluster, "neighbours": neighbours, "orientation": orientation, "stiffness": stiffness, "jacobians": jacobians, "flux_local": flux_local, "flux_neigh": flux_neigh, "flux_plus": flux_plus, "flux_minus": flux_minus}


step_length = 0.2


def per_element(matrix, values):
    total = matrix[:, 0][:, None, :] * values[0][None, :, :]
    for inner in range(1, matrix.shape[1]):
        total = total + matrix[:, inner][:, None, :] * values[inner][None, :, :]
    return total


def per_element_basis(matrix, values):
    total = matrix[None, :, 0, :] * values[:, 0][:, None, :]
    for inner in range(1, matrix.shape[1]):
        total = total + matrix[None, :, inner, :] * values[:, inner][:, None, :]
    return total


def apply_star(values, stiffness, geometry, element_jac, transpose):
    pattern = "ba,vbe->vae" if transpose else "ab,vbe->vae"
    mapped = [jnp.einsum(pattern, stiffness[direction], values, precision=lax.Precision.HIGHEST) for direction in range(3)]
    summed = jnp.zeros_like(values)
    for column in range(3):
        mixture = mapped[0] * geometry[0, column] + mapped[1] * geometry[1, column] + mapped[2] * geometry[2, column]
        summed = summed + per_element(element_jac[column], mixture)
    return summed


def predict(values, stiffness, geometry, element_jac, coarse, shifted):
    first = -apply_star(values, stiffness, geometry, element_jac, False)
    second = -apply_star(first, stiffness, geometry, element_jac, False)
    if shifted:
        values = values + coarse * (step_length * first + 0.5 * step_length ** 2 * second)
        first = first + coarse * (step_length * second)
    return step_length * values + (step_length ** 2 / 2) * first + (step_length ** 3 / 6) * second


def update(own, neighbour_parts, face_scale, stiffness, geometry, element_jac, element_plus, element_minus, face_neigh, flux_local):
    result = apply_star(own, stiffness, geometry, element_jac, True)
    plus = per_element(element_plus, own)
    for face in range(4):
        minus = per_element(element_minus, neighbour_parts[face])
        across = jnp.einsum("ab,vbe->vae", flux_local[face], plus, precision=lax.Precision.HIGHEST)
        across = across + per_element_basis(face_neigh[face], minus)
        result = result - face_scale[face] * across
    return result


def element_tables(material, orientation, jacobians, flux_plus, flux_minus, flux_neigh):
    medium_mask = (material[None, :] == jnp.arange(3, dtype=jnp.int32)[:, None]).astype(jnp.float32)
    element_jac = jnp.einsum("mcvw,me->cvwe", jacobians, medium_mask, precision=lax.Precision.HIGHEST)
    element_plus = jnp.einsum("mvw,me->vwe", flux_plus, medium_mask, precision=lax.Precision.HIGHEST)
    element_minus = jnp.einsum("mvw,me->vwe", flux_minus, medium_mask, precision=lax.Precision.HIGHEST)
    turns = jnp.arange(12, dtype=jnp.int32)[:, None]
    face_neigh = [jnp.einsum("tab,te->abe", flux_neigh, (orientation[face][None, :] == turns).astype(jnp.float32), precision=lax.Precision.HIGHEST) for face in range(4)]
    return element_jac, element_plus, element_minus, face_neigh


def global_index(neighbours):
    glob = jnp.arange(ELEMENTS, dtype=jnp.int32)
    owner = glob // ELEM_DEV
    dom_index = owner // N_SUB
    sub_index = owner % N_SUB
    sub_start = ELEM_DEV
    left_start = ELEM_DEV + N_SUB * SUB_COPY
    right_start = left_start + COPY_DEV
    local_glob = owner * ELEM_DEV + neighbours
    offset = neighbours - sub_start
    sub_glob = (dom_index * N_SUB + offset // SUB_COPY) * ELEM_DEV + offset % SUB_COPY
    left_glob = (jnp.mod(dom_index - 1, N_DOM) * N_SUB + sub_index) * ELEM_DEV + ELEM_DEV - COPY_DEV + (neighbours - left_start)
    right_glob = (jnp.mod(dom_index + 1, N_DOM) * N_SUB + sub_index) * ELEM_DEV + (neighbours - right_start)
    result = jnp.where(neighbours < sub_start, local_glob, sub_glob)
    result = jnp.where(neighbours >= left_start, left_glob, result)
    result = jnp.where(neighbours >= right_start, right_glob, result)
    return result.astype(jnp.int32)


def reference(state, geometry, face_scale, material, cluster, neighbours, orientation, stiffness, jacobians, flux_local, flux_neigh, flux_plus, flux_minus):
    element_jac, element_plus, element_minus, face_neigh = element_tables(material, orientation, jacobians, flux_plus, flux_minus, flux_neigh)
    coarse = cluster.astype(jnp.float32)
    finer = 1.0 - coarse
    indices = global_index(neighbours)

    def advance(integral):
        parts = [jnp.take(integral, indices[face], axis=2) for face in range(4)]
        return update(integral, parts, face_scale, stiffness, geometry, element_jac, element_plus, element_minus, face_neigh, flux_local)

    for outer_step in range(MACRO):
        first_change = advance(predict(state, stiffness, geometry, element_jac, coarse, False))
        middle = state + finer * first_change
        second_change = advance(predict(middle, stiffness, geometry, element_jac, coarse, True))
        state = middle + finer * second_change + coarse * (first_change + second_change)
    return state
```

```python
import functools

import jax
import jax.numpy as jnp
from jax import lax
from jax.experimental import pallas as pl
from jax.experimental.pallas import tpu as pltpu
from jax.sharding import PartitionSpec as P

COPY_DEV = 128
SUB_COPY = 64
QUANT = 9
BASIS = 10
GROUP = 32
ROWS = 96
BLOCKS = 5
WIDE = 512

step_length = 0.2
f32 = jnp.float32
bf16 = jnp.bfloat16
MESH = pl.DeviceIdType.MESH


def iota(shape, dim):
    return lax.broadcasted_iota(jnp.int32, shape, dim)


def place(row):
    inner = row & (GROUP - 1)
    third = (inner >= BASIS).astype(jnp.int32) + (inner >= 2 * BASIS).astype(jnp.int32)
    quantity = 3 * lax.shift_right_logical(row, 5) + third
    return quantity, third, inner - BASIS * third, inner < 3 * BASIS


def split(values):
    high = values.astype(bf16)
    return high, (values - high.astype(f32)).astype(bf16)


def mul(a, b):
    return jnp.dot(a, b, preferred_element_type=f32)


def row_of(quantity):
    return GROUP * (quantity // 3) + BASIS * (quantity % 3)


def kernel(
    n_dom,
    n_sub,
    state_ref,
    geometry_ref,
    scale_ref,
    material_ref,
    cluster_ref,
    neighbours_ref,
    orientation_ref,
    stiffness_ref,
    jacobians_ref,
    local_ref,
    neigh_ref,
    plus_ref,
    minus_ref,
    out_ref,
    dofs,
    small,
    tiled,
    basis,
    fluxes,
    wide_high,
    wide_low,
    right_high,
    right_low,
    hot,
    table,
    picked_high,
    picked_low,
    ends,
    packed,
    from_sub,
    from_dom,
    send_sem,
    recv_sem,
):
    count = state_ref.shape[2]
    dom, sub = lax.axis_index("dom"), lax.axis_index("sub")
    left = (lax.rem(dom + n_dom - 1, n_dom), sub)
    right = (lax.rem(dom + 1, n_dom), sub)
    peers = [(dom, lax.rem(sub + k, n_sub)) for k in range(1, n_sub)]

    barrier = pltpu.get_barrier_semaphore()
    for other in [left, right] + peers:
        pl.semaphore_signal(barrier, inc=1, device_id=other, device_id_type=MESH)

    small[...] = jnp.zeros_like(small)
    for i in range(3):
        small[i, :BASIS, :BASIS] = stiffness_ref[i]
    for i in range(4):
        small[6 + i, :BASIS, :BASIS] = local_ref[i]
    for i in range(12):
        small[10 + i, :BASIS, :BASIS] = neigh_ref[i]
    col = iota((16, ROWS), 1)
    _, _, fn, ok = place(col)
    hit = (iota((16, ROWS), 0) == fn) & ok
    pick_high = jnp.where(hit & (col < 2 * GROUP), 1.0, 0.0).astype(bf16)
    pick_low = jnp.where(hit & (col >= 2 * GROUP), 1.0, 0.0).astype(bf16)
    for i in range(3):
        small[3 + i, :, :16] = small[i][:, :16].T
    high, low = split(small[...].reshape(22 * 16, 128)[:, :16])
    spread = (mul(high, pick_high) + mul(low, pick_low)).reshape(22, 16, ROWS)
    tiled[...] = jnp.zeros_like(tiled)
    for third in range(3):
        tiled[:, BASIS * third : BASIS * third + BASIS, :] = spread[:, :BASIS, :]
    shape = (22, GROUP, ROWS)
    _, third_row, _, ok_row = place(iota(shape, 1))
    _, third_col, _, ok_col = place(iota(shape, 2) & (GROUP - 1))
    keep = (third_row == third_col) & ok_row & ok_col
    basis[...] = jnp.where(keep, tiled[...], 0.0).astype(bf16).reshape(22 * GROUP, ROWS)

    fluxes[...] = jnp.zeros_like(fluxes)
    for m in range(3):
        for c in range(3):
            fluxes[c, m, :QUANT, :QUANT] = jacobians_ref[m, c]
        fluxes[3, m, :QUANT, :QUANT] = -plus_ref[m]
        fluxes[4, m, :QUANT, :QUANT] = -minus_ref[m]
    high, low = split(fluxes[...].reshape(BLOCKS * 48, 128)[:, :16])
    rows_high, rows_low = 0.0, 0.0
    for k in range(BLOCKS):
        col = iota((16, WIDE), 1) - ROWS * k
        quantity, _, _, ok = place(col & 127)
        hit = (col >= 0) & (col < ROWS) & ok & (quantity == iota((16, WIDE), 0))
        pick = jnp.where(hit, 1.0, 0.0).astype(bf16)
        rows_high = rows_high + mul(high[48 * k : 48 * k + 48], pick)
        rows_low = rows_low + mul(low[48 * k : 48 * k + 48], pick)
    quantity, _, fn_row, ok_row = place(iota((ROWS, WIDE), 0))
    _, _, fn_col, ok_col = place(iota((ROWS, WIDE), 1))
    keep = (fn_row == fn_col) & ok_row & ok_col & (iota((ROWS, WIDE), 1) < BLOCKS * ROWS)
    quantity, _, _, ok = place(iota((ROWS, 16), 0))
    pick = jnp.where((quantity == iota((ROWS, 16), 1)) & ok, 1.0, 0.0).astype(bf16)
    rows_high, rows_low = rows_high.astype(bf16), rows_low.astype(bf16)
    for m in range(3):
        whole = mul(pick, rows_high[16 * m : 16 * m + 16])
        wide_high[ROWS * m : ROWS * m + ROWS, :] = jnp.where(keep, whole, 0.0).astype(bf16)
        whole = mul(pick, rows_low[16 * m : 16 * m + 16])
        wide_low[ROWS * m : ROWS * m + ROWS, :] = jnp.where(keep, whole, 0.0).astype(bf16)

    pad = jnp.zeros((WIDE - BLOCKS * ROWS, count), bf16)
    right_high[BLOCKS * ROWS :, :] = pad
    right_low[BLOCKS * ROWS :, :] = pad

    dofs[...] = jnp.zeros_like(dofs)
    for v in range(QUANT):
        dofs[row_of(v) : row_of(v) + BASIS, :] = state_ref[v]

    material = jnp.broadcast_to(material_ref[...], (ROWS, count))
    coarse = jnp.broadcast_to(cluster_ref[...], (ROWS, count)).astype(f32)

    def on_basis(high, low, first, last):
        parts = []
        for g in range(3):
            h, l = high[GROUP * g : GROUP * g + GROUP], low[GROUP * g : GROUP * g + GROUP]
            parts.append(mul(basis[GROUP * first : GROUP * last, :], jnp.concatenate([h, l, h], axis=0)))
        return [
            jnp.concatenate([part[GROUP * k : GROUP * k + GROUP] for part in parts], axis=0)
            for k in range(last - first)
        ]

    def mixtures(mapped):
        for c in range(3):
            mixture = (
                mapped[0] * geometry_ref[0, c : c + 1, :]
                + mapped[1] * geometry_ref[1, c : c + 1, :]
                + mapped[2] * geometry_ref[2, c : c + 1, :]
            )
            h, l = split(mixture)
            right_high[ROWS * c : ROWS * c + ROWS, :] = h
            right_low[ROWS * c : ROWS * c + ROWS, :] = l

    def on_quantities(depth):
        every = (
            mul(wide_high[:, :depth], right_high[:depth, :])
            + mul(wide_high[:, :depth], right_low[:depth, :])
            + mul(wide_low[:, :depth], right_high[:depth, :])
        )
        return jnp.where(
            material == 0,
            every[:ROWS],
            jnp.where(material == 1, every[ROWS : 2 * ROWS], every[2 * ROWS :]),
        )

    def star(values):
        high, low = split(values)
        mixtures(on_basis(high, low, 0, 3))
        return on_quantities(3 * ROWS)

    def predict(values, shifted):
        first = -star(values)
        second = -star(first)
        if shifted:
            values = values + coarse * (step_length * first + 0.5 * step_length**2 * second)
            first = first + coarse * (step_length * second)
        return step_length * values + step_length**2 / 2 * first + step_length**3 / 6 * second

    def halves(values, lanes):
        high, low = split(values)
        table[:ROWS, lanes] = high
        table[ROWS:, lanes] = low

    lane = iota((ROWS // 2, COPY_DEV), 1)
    front = lane < SUB_COPY

    def send(integral, r):
        ends[r, 0] = integral[:, :COPY_DEV]
        ends[r, 1] = integral[:, count - COPY_DEV :]
        top, bottom = integral[: ROWS // 2, :COPY_DEV], integral[ROWS // 2 :, :COPY_DEV]
        mine = jnp.where(front, top, pltpu.roll(bottom, SUB_COPY, 1))
        packed[r] = mine
        from_sub[r, sub] = mine
        if r == 0:
            pl.semaphore_wait(barrier, n_sub + 1)
        copies = []
        for k, (end, other) in enumerate([(1, right), (0, left)]):
            copies.append(
                pltpu.make_async_remote_copy(
                    src_ref=ends.at[r, end],
                    dst_ref=from_dom.at[r, k],
                    send_sem=send_sem.at[r, k],
                    recv_sem=recv_sem.at[r, k],
                    device_id=other,
                    device_id_type=MESH,
                )
            )
        for k, other in enumerate(peers):
            copies.append(
                pltpu.make_async_remote_copy(
                    src_ref=packed.at[r],
                    dst_ref=from_sub.at[r, sub],
                    send_sem=send_sem.at[r, 2 + k],
                    recv_sem=recv_sem.at[r, 2 + k],
                    device_id=other,
                    device_id_type=MESH,
                )
            )
        for copy in copies:
            copy.start()
        return copies

    depth = hot.shape[0]

    def advance(values, r):
        integral = predict(values, r == 1)
        copies = send(integral, r)
        if r == 0:
            for f in range(4):
                wanted = jnp.broadcast_to(neighbours_ref[f : f + 1, :], (depth, count))
                hit = jnp.where(iota((depth, count), 0) == wanted, 1.0, 0.0)
                hot[:, count * f : count * f + count] = hit.astype(bf16)
        high, low = split(integral)
        table[:ROWS, :count] = high
        table[ROWS:, :count] = low
        mapped = on_basis(high, low, 3, 10)
        mixtures(mapped[:3])
        local = mapped[3] * scale_ref[0:1, :]
        for f in range(1, 4):
            local = local + mapped[3 + f] * scale_ref[f : f + 1, :]
        h, l = split(local)
        right_high[3 * ROWS : 4 * ROWS, :] = h
        right_low[3 * ROWS : 4 * ROWS, :] = l

        for copy in copies:
            copy.wait()
        for pair in range(n_sub // 2):
            one, two = from_sub[r, 2 * pair], from_sub[r, 2 * pair + 1]
            top = jnp.where(front, one, pltpu.roll(two, SUB_COPY, 1))
            bottom = jnp.where(front, pltpu.roll(one, SUB_COPY, 1), two)
            lanes = slice(count + 128 * pair, count + 128 * pair + 128)
            halves(jnp.concatenate([top, bottom], axis=0), lanes)
        for k in range(2):
            start = count + SUB_COPY * n_sub + COPY_DEV * k
            halves(from_dom[r, k], slice(start, start + COPY_DEV))

        for f in range(4):
            lanes = slice(count * f, count * f + count)
            found = mul(table[...], hot[:, lanes])
            picked_high[:, lanes] = found[:ROWS].astype(bf16)
            picked_low[:, lanes] = found[ROWS:].astype(bf16)
        for g in range(3):
            rows = slice(GROUP * g, GROUP * g + GROUP)
            total = 0.0
            for f in range(4):
                lanes = slice(count * f, count * f + count)
                h, l = picked_high[rows, lanes], picked_low[rows, lanes]
                turned = mul(basis[10 * GROUP :, :], jnp.concatenate([h, l, h], axis=0))
                turn = jnp.broadcast_to(orientation_ref[f : f + 1, :], (GROUP, count))
                chosen = turned[:GROUP]
                for t in range(1, 12):
                    chosen = jnp.where(turn == t, turned[GROUP * t : GROUP * t + GROUP], chosen)
                total = total + chosen * scale_ref[f : f + 1, :]
            h, l = split(total)
            right_high[4 * ROWS + GROUP * g : 4 * ROWS + GROUP * g + GROUP, :] = h
            right_low[4 * ROWS + GROUP * g : 4 * ROWS + GROUP * g + GROUP, :] = l
        return on_quantities(WIDE)

    state = dofs[...]
    first_change = advance(state, 0)
    middle = state + (1.0 - coarse) * first_change
    second_change = advance(middle, 1)
    dofs[...] = middle + second_change + coarse * first_change
    for v in range(QUANT):
        out_ref[v] = dofs[row_of(v) : row_of(v) + BASIS, :]


def shards(n_dom, n_sub, state, geometry, face_scale, material, cluster, *rest):
    count = state.shape[2]
    depth = count + SUB_COPY * n_sub + 2 * COPY_DEV
    vmem = pl.BlockSpec(memory_space=pltpu.VMEM)
    copies = n_sub + 1
    return pl.pallas_call(
        functools.partial(kernel, n_dom, n_sub),
        out_shape=jax.ShapeDtypeStruct(state.shape, f32),
        in_specs=[vmem] * 13,
        out_specs=vmem,
        scratch_shapes=[
            pltpu.VMEM((ROWS, count), f32),
            pltpu.VMEM((22, 16, 128), f32),
            pltpu.VMEM((22, GROUP, ROWS), f32),
            pltpu.VMEM((22 * GROUP, ROWS), bf16),
            pltpu.VMEM((BLOCKS, 3, 16, 128), f32),
            pltpu.VMEM((3 * ROWS, WIDE), bf16),
            pltpu.VMEM((3 * ROWS, WIDE), bf16),
            pltpu.VMEM((WIDE, count), bf16),
            pltpu.VMEM((WIDE, count), bf16),
            pltpu.VMEM((depth, 4 * count), bf16),
            pltpu.VMEM((2 * ROWS, depth), bf16),
            pltpu.VMEM((ROWS, 4 * count), bf16),
            pltpu.VMEM((ROWS, 4 * count), bf16),
            pltpu.VMEM((2, 2, ROWS, COPY_DEV), f32),
            pltpu.VMEM((2, ROWS // 2, COPY_DEV), f32),
            pltpu.VMEM((2, n_sub, ROWS // 2, COPY_DEV), f32),
            pltpu.VMEM((2, 2, ROWS, COPY_DEV), f32),
            pltpu.SemaphoreType.DMA((2, copies)),
            pltpu.SemaphoreType.DMA((2, copies)),
        ],
        compiler_params=pltpu.CompilerParams(
            collective_id=0, has_side_effects=True, vmem_limit_bytes=48 * 1024 * 1024
        ),
    )(state, geometry, face_scale, material[None], cluster[None], *rest)


def solution(mesh):
    placed = (
        P(None, None, ("dom", "sub")),
        P(None, None, ("dom", "sub")),
        P(None, ("dom", "sub")),
        P(("dom", "sub")),
        P(("dom", "sub")),
        P(None, ("dom", "sub")),
        P(None, ("dom", "sub")),
        P(),
        P(),
        P(),
        P(),
        P(),
        P(),
    )
    return jax.shard_map(
        functools.partial(shards, mesh.shape["dom"], mesh.shape["sub"]),
        mesh=mesh,
        in_specs=placed,
        out_specs=P(None, None, ("dom", "sub")),
        check_vma=False,
    )
```

```python
import functools

import jax
import jax.numpy as jnp
from jax import lax
from jax.experimental import pallas as pl
from jax.experimental.pallas import tpu as pltpu
from jax.sharding import PartitionSpec as P

COPY_DEV = 128
SUB_COPY = 64
QUANT = 9
BASIS = 10
GROUP = 32
ROWS = 96
SLOTS = 24
LIMIT = 62 * 1024 * 1024

step_length = 0.2
f32 = jnp.float32
bf16 = jnp.bfloat16
MESH = pl.DeviceIdType.MESH


def iota(shape, dim):
    return lax.broadcasted_iota(jnp.int32, shape, dim)


def place(row):
    inner = row & (GROUP - 1)
    third = (inner >= BASIS).astype(jnp.int32) + (inner >= 2 * BASIS).astype(jnp.int32)
    quantity = 3 * lax.shift_right_logical(row, 5) + third
    return quantity, third, inner - BASIS * third, inner < 3 * BASIS


def split(values):
    high = values.astype(bf16)
    return high, (values - high.astype(f32)).astype(bf16)


def mul(a, b):
    return jnp.dot(a, b, preferred_element_type=f32)


def row_of(quantity):
    return GROUP * (quantity // 3) + BASIS * (quantity % 3)


def kernel(n_dom, n_sub, *refs):
    inputs, out_ref, scratch = refs[:13], refs[13], refs[14:]
    held, scratch = scratch[:13], scratch[13:]
    (
        state_ref,
        geometry_ref,
        scale_ref,
        material_ref,
        cluster_ref,
        neighbours_ref,
        orientation_ref,
        stiffness_ref,
        jacobians_ref,
        local_ref,
        neigh_ref,
        plus_ref,
        minus_ref,
    ) = held
    (
        dofs,
        small,
        basis,
        fluxes,
        wide,
        right,
        hot,
        table,
        own,
        picked_high,
        picked_low,
        ends,
        packed,
        from_sub,
        from_dom,
        load_sem,
        send_sem,
        recv_sem,
    ) = scratch
    count = state_ref.shape[2]
    dom, sub = lax.axis_index("dom"), lax.axis_index("sub")
    left_dev = (lax.rem(dom + n_dom - 1, n_dom), sub)
    right_dev = (lax.rem(dom + 1, n_dom), sub)
    peers = [(dom, lax.rem(sub + k, n_sub)) for k in range(1, n_sub)]

    barrier = pltpu.get_barrier_semaphore()
    for other in [left_dev, right_dev] + peers:
        pl.semaphore_signal(barrier, inc=1, device_id=other, device_id_type=MESH)
    loads = [pltpu.make_async_copy(inputs[i], held[i], load_sem.at[i]) for i in range(13)]
    for i in (7, 8, 0, 1, 3, 4, 2, 5, 6, 9, 10, 11, 12):
        loads[i].start()

    small[...] = jnp.zeros_like(small)
    fluxes[...] = jnp.zeros_like(fluxes)
    right[...] = jnp.zeros_like(right)
    dofs[...] = jnp.zeros_like(dofs)
    col = iota((16, ROWS), 1)
    _, _, fn, ok = place(col)
    hit = (iota((16, ROWS), 0) == fn) & ok
    pick_high = jnp.where(hit & (col < 2 * GROUP), 1.0, 0.0).astype(bf16)
    pick_low = jnp.where(hit & (col >= 2 * GROUP), 1.0, 0.0).astype(bf16)
    _, third_row, fn_row, ok_row = place(iota((GROUP, ROWS), 0))
    _, third_col, _, ok_col = place(iota((GROUP, ROWS), 1) & (GROUP - 1))
    same_third = (third_row == third_col) & ok_row & ok_col
    _, _, fn, ok = place(iota((GROUP, SLOTS * BASIS), 0))
    offset = jnp.where(ok, iota((GROUP, SLOTS * BASIS), 1) - SLOTS * fn, -1)

    def expand(spread, first, last):
        chosen = [jnp.where(offset == k, 1.0, 0.0).astype(bf16) for k in range(first, last)]
        full = mul(jnp.concatenate(chosen, axis=0), spread)
        for k in range(first, last):
            block = full[GROUP * (k - first) : GROUP * (k - first) + GROUP]
            basis[GROUP * k : GROUP * k + GROUP, :] = jnp.where(same_third, block, 0.0).astype(bf16)

    col = iota((16, 128), 1)
    quantity, _, _, ok = place(col)
    pick = jnp.where((quantity == iota((16, 128), 0)) & ok & (col < ROWS), 1.0, 0.0).astype(bf16)
    _, _, fn_row, ok_row = place(iota((ROWS, 128), 0))
    _, _, fn_col, ok_col = place(iota((ROWS, 128), 1))
    same_fn = (fn_row == fn_col) & ok_row & ok_col & (iota((ROWS, 128), 1) < ROWS)
    quantity, _, _, ok = place(iota((ROWS, 16 * QUANT), 0))
    flux_offset = jnp.where(ok, iota((ROWS, 16 * QUANT), 1) - 16 * quantity, -1)

    def expand_fluxes(slots, blocks):
        high, low = split(fluxes[...].reshape(16 * QUANT, 128)[:, :16])
        spread_high, spread_low = mul(high, pick).astype(bf16), mul(low, pick).astype(bf16)
        spread = jnp.concatenate([spread_high, spread_low], axis=1)
        for m in range(3):
            chosen = [jnp.where(flux_offset == slot[m], 1.0, 0.0).astype(bf16) for slot in slots]
            full = mul(jnp.concatenate(chosen, axis=0), spread)
            for i, (one, two, three) in enumerate(blocks):
                part = full[ROWS * i : ROWS * i + ROWS]
                high = jnp.where(same_fn, part[:, :128], 0.0).astype(bf16)
                low = jnp.where(same_fn, part[:, 128:], 0.0).astype(bf16)
                rows = slice(ROWS * m, ROWS * m + ROWS)
                wide[rows, 128 * one : 128 * one + 128] = high
                wide[rows, 128 * two : 128 * two + 128] = high
                wide[rows, 128 * three : 128 * three + 128] = low

    loads[7].wait()
    small[:, :3, :BASIS] = stiffness_ref[...]
    high, low = split(small[...].reshape(SLOTS * BASIS, 128)[:, :16])
    expand((mul(high, pick_high) + mul(low, pick_low)).astype(bf16), 0, 3)

    loads[8].wait()
    for m in range(3):
        fluxes[:, 3 * m : 3 * m + 3, :QUANT] = jacobians_ref[m]
    expand_fluxes([(c, 3 + c, 6 + c) for c in range(3)], [(c, 3 + c, 6 + c) for c in range(3)])

    loads[0].wait()
    for v in range(QUANT):
        dofs[row_of(v) : row_of(v) + BASIS, :] = state_ref[v]
    for i in (1, 3, 4):
        loads[i].wait()
    material = jnp.broadcast_to(material_ref[...], (ROWS, count))
    coarse = jnp.broadcast_to(cluster_ref[...], (ROWS, count)).astype(f32)

    def on_basis(high, low, first, last):
        parts = []
        for g in range(3):
            h, l = high[GROUP * g : GROUP * g + GROUP], low[GROUP * g : GROUP * g + GROUP]
            parts.append(mul(basis[GROUP * first : GROUP * last, :], jnp.concatenate([h, l, h], axis=0)))
        return [
            jnp.concatenate([part[GROUP * k : GROUP * k + GROUP] for part in parts], axis=0)
            for k in range(last - first)
        ]

    def put(values, blocks, start, length):
        high, low = split(values)
        for block, half in zip(blocks, (high, low, high)):
            right[128 * block + start : 128 * block + start + length, :] = half

    def mixtures(mapped):
        for c in range(3):
            mixture = (
                mapped[0] * geometry_ref[0, c : c + 1, :]
                + mapped[1] * geometry_ref[1, c : c + 1, :]
                + mapped[2] * geometry_ref[2, c : c + 1, :]
            )
            put(mixture, (c, 3 + c, 6 + c), 0, ROWS)

    def on_quantities(first, last):
        every = mul(wide[:, 128 * first : 128 * last], right[128 * first : 128 * last, :])
        return jnp.where(
            material == 0,
            every[:ROWS],
            jnp.where(material == 1, every[ROWS : 2 * ROWS], every[2 * ROWS :]),
        )

    def star(values):
        high, low = split(values)
        mixtures(on_basis(high, low, 0, 3))
        return on_quantities(0, 9)

    def predict(values, shifted):
        first = -star(values)
        second = -star(first)
        if shifted:
            values = values + coarse * (step_length * first + 0.5 * step_length**2 * second)
            first = first + coarse * (step_length * second)
        return step_length * values + step_length**2 / 2 * first + step_length**3 / 6 * second

    def halves(values, lanes):
        high, low = split(values)
        table[:ROWS, lanes] = high
        table[ROWS:, lanes] = low

    lane = iota((ROWS // 2, COPY_DEV), 1)
    front = lane < SUB_COPY

    def send(integral, r):
        ends[r, 0] = integral[:, :COPY_DEV]
        ends[r, 1] = integral[:, count - COPY_DEV :]
        top, bottom = integral[: ROWS // 2, :COPY_DEV], integral[ROWS // 2 :, :COPY_DEV]
        mine = jnp.where(front, top, pltpu.roll(bottom, SUB_COPY, 1))
        packed[r] = mine
        from_sub[r, sub] = mine
        if r == 0:
            pl.semaphore_wait(barrier, n_sub + 1)
        copies = []
        for k, (end, other) in enumerate([(1, right_dev), (0, left_dev)]):
            copies.append(
                pltpu.make_async_remote_copy(
                    src_ref=ends.at[r, end],
                    dst_ref=from_dom.at[r, k],
                    send_sem=send_sem.at[r, k],
                    recv_sem=recv_sem.at[r, k],
                    device_id=other,
                    device_id_type=MESH,
                )
            )
        for k, other in enumerate(peers):
            copies.append(
                pltpu.make_async_remote_copy(
                    src_ref=packed.at[r],
                    dst_ref=from_sub.at[r, sub],
                    send_sem=send_sem.at[r, 2 + k],
                    recv_sem=recv_sem.at[r, 2 + k],
                    device_id=other,
                    device_id_type=MESH,
                )
            )
        for copy in copies:
            copy.start()
        return copies

    depth = hot.shape[0]

    def prepare():
        for i in (2, 5, 6, 9, 10, 11, 12):
            loads[i].wait()
        for f in range(4):
            wanted = jnp.broadcast_to(neighbours_ref[f : f + 1, :], (depth, count))
            hit = jnp.where(iota((depth, count), 0) == wanted, 1.0, 0.0)
            hot[:, count * f : count * f + count] = hit.astype(bf16)
        small[:, 6:10, :BASIS] = local_ref[...]
        small[:, 10:22, :BASIS] = neigh_ref[...]
        high, low = split(small[...].reshape(SLOTS * BASIS, 128)[:, :16])
        expand((mul(high, pick_high) + mul(low, pick_low)).astype(bf16), 6, 22)
        which = iota((16, SLOTS * BASIS), 1) - SLOTS * iota((16, SLOTS * BASIS), 0)
        _, _, fn, ok = place(iota((GROUP, 16), 0))
        repeat = jnp.where((fn == iota((GROUP, 16), 1)) & ok, 1.0, 0.0).astype(bf16)
        for k in range(3):
            chosen = jnp.where(which == k, 1.0, 0.0).astype(bf16)
            h, l = mul(chosen, high).T.astype(bf16), mul(chosen, low).T.astype(bf16)
            block = mul(repeat, (mul(h, pick_high) + mul(l, pick_low)).astype(bf16))
            rows = slice(GROUP * (3 + k), GROUP * (4 + k))
            basis[rows, :] = jnp.where(same_third, block, 0.0).astype(bf16)
        fluxes[:, 9:12, :QUANT] = -plus_ref[...]
        fluxes[:, 12:15, :QUANT] = -minus_ref[...]
        expand_fluxes([(9, 10, 11), (12, 13, 14)], [(9, 10, 11), (12, 13, 14)])

    def advance(values, r):
        integral = predict(values, r == 1)
        copies = send(integral, r)
        if r == 0:
            prepare()
        high, low = split(integral)
        table[:ROWS, :count] = high
        table[ROWS:, :count] = low
        mapped = on_basis(high, low, 3, 10)
        mixtures(mapped[:3])
        local = mapped[3] * scale_ref[0:1, :]
        for f in range(1, 4):
            local = local + mapped[3 + f] * scale_ref[f : f + 1, :]
        put(local, (9, 10, 11), 0, ROWS)
        change = on_quantities(0, 12)
        for f in range(4):
            lanes = slice(count * f, count * f + count)
            own[:, lanes] = mul(table[:, :count], hot[:count, lanes]).astype(bf16)

        for copy in copies:
            copy.wait()
        for pair in range(n_sub // 2):
            one, two = from_sub[r, 2 * pair], from_sub[r, 2 * pair + 1]
            top = jnp.where(front, one, pltpu.roll(two, SUB_COPY, 1))
            bottom = jnp.where(front, pltpu.roll(one, SUB_COPY, 1), two)
            lanes = slice(count + 128 * pair, count + 128 * pair + 128)
            halves(jnp.concatenate([top, bottom], axis=0), lanes)
        for k in range(2):
            start = count + SUB_COPY * n_sub + COPY_DEV * k
            halves(from_dom[r, k], slice(start, start + COPY_DEV))

        totals = [0.0] * 3
        for f in range(4):
            lanes = slice(count * f, count * f + count)
            found = mul(table[:, count:], hot[count:, lanes]).astype(bf16) + own[:, lanes]
            picked_high[:, lanes] = found[:ROWS]
            picked_low[:, lanes] = found[ROWS:]
            for g in range(3):
                rows = slice(GROUP * g, GROUP * g + GROUP)
                h, l = picked_high[rows, lanes], picked_low[rows, lanes]
                turned = mul(basis[10 * GROUP :, :], jnp.concatenate([h, l, h], axis=0))
                turn = jnp.broadcast_to(orientation_ref[f : f + 1, :], (GROUP, count))
                chosen = turned[:GROUP]
                for t in range(1, 12):
                    chosen = jnp.where(turn == t, turned[GROUP * t : GROUP * t + GROUP], chosen)
                totals[g] = totals[g] + chosen * scale_ref[f : f + 1, :]
        for g in range(3):
            put(totals[g], (12, 13, 14), GROUP * g, GROUP)
        return change + on_quantities(12, 15)

    state = dofs[...]
    first_change = advance(state, 0)
    middle = state + (1.0 - coarse) * first_change
    second_change = advance(middle, 1)
    dofs[...] = middle + second_change + coarse * first_change
    for v in range(QUANT):
        out_ref[v] = dofs[row_of(v) : row_of(v) + BASIS, :]


def shards(n_dom, n_sub, state, geometry, face_scale, material, cluster, neighbours, orientation, *parameters):
    stiffness, jacobians, flux_local, flux_neigh, flux_plus, flux_minus = parameters
    count = state.shape[2]
    depth = count + SUB_COPY * n_sub + 2 * COPY_DEV
    operands = [
        state,
        geometry,
        face_scale,
        material[None],
        cluster[None],
        neighbours,
        orientation,
        stiffness.transpose(1, 0, 2),
        jacobians.transpose(0, 2, 1, 3),
        flux_local.transpose(1, 0, 2),
        flux_neigh.transpose(1, 0, 2),
        flux_plus.transpose(1, 0, 2),
        flux_minus.transpose(1, 0, 2),
    ]
    copies = n_sub + 1
    return pl.pallas_call(
        functools.partial(kernel, n_dom, n_sub),
        out_shape=jax.ShapeDtypeStruct(state.shape, f32),
        in_specs=[pl.BlockSpec(memory_space=pltpu.HBM)] * 13,
        out_specs=pl.BlockSpec(memory_space=pltpu.VMEM),
        scratch_shapes=[pltpu.VMEM(x.shape, x.dtype) for x in operands]
        + [
            pltpu.VMEM((ROWS, count), f32),
            pltpu.VMEM((BASIS, SLOTS, 128), f32),
            pltpu.VMEM((22 * GROUP, ROWS), bf16),
            pltpu.VMEM((QUANT, 16, 128), f32),
            pltpu.VMEM((3 * ROWS, 15 * 128), bf16),
            pltpu.VMEM((15 * 128, count), bf16),
            pltpu.VMEM((depth, 4 * count), bf16),
            pltpu.VMEM((2 * ROWS, depth), bf16),
            pltpu.VMEM((2 * ROWS, 4 * count), bf16),
            pltpu.VMEM((ROWS, 4 * count), bf16),
            pltpu.VMEM((ROWS, 4 * count), bf16),
            pltpu.VMEM((2, 2, ROWS, COPY_DEV), f32),
            pltpu.VMEM((2, ROWS // 2, COPY_DEV), f32),
            pltpu.VMEM((2, n_sub, ROWS // 2, COPY_DEV), f32),
            pltpu.VMEM((2, 2, ROWS, COPY_DEV), f32),
            pltpu.SemaphoreType.DMA((13,)),
            pltpu.SemaphoreType.DMA((2, copies)),
            pltpu.SemaphoreType.DMA((2, copies)),
        ],
        compiler_params=pltpu.CompilerParams(
            collective_id=0, has_side_effects=True, vmem_limit_bytes=LIMIT
        ),
    )(*operands)


def solution(mesh):
    placed = (
        P(None, None, ("dom", "sub")),
        P(None, None, ("dom", "sub")),
        P(None, ("dom", "sub")),
        P(("dom", "sub")),
        P(("dom", "sub")),
        P(None, ("dom", "sub")),
        P(None, ("dom", "sub")),
        P(),
        P(),
        P(),
        P(),
        P(),
        P(),
    )
    return jax.shard_map(
        functools.partial(shards, mesh.shape["dom"], mesh.shape["sub"]),
        mesh=mesh,
        in_specs=placed,
        out_specs=P(None, None, ("dom", "sub")),
        check_vma=False,
    )
```

```python
import functools

import jax
import jax.numpy as jnp
from jax import lax
from jax.experimental import pallas as pl
from jax.experimental.pallas import tpu as pltpu
from jax.sharding import PartitionSpec as P

COPY_DEV = 128
SUB_COPY = 64
QUANT = 9
BASIS = 10
GROUP = 32
ROWS = 96
SLOTS = 24
LIMIT = 56 * 1024 * 1024

step_length = 0.2
f32 = jnp.float32
bf16 = jnp.bfloat16
MESH = pl.DeviceIdType.MESH


def iota(shape, dim):
    return lax.broadcasted_iota(jnp.int32, shape, dim)


def place(row):
    inner = row & (GROUP - 1)
    third = (inner >= BASIS).astype(jnp.int32) + (inner >= 2 * BASIS).astype(jnp.int32)
    quantity = 3 * lax.shift_right_logical(row, 5) + third
    return quantity, third, inner - BASIS * third, inner < 3 * BASIS


def split(values):
    high = values.astype(bf16)
    return high, (values - high.astype(f32)).astype(bf16)


def mul(a, b):
    return jnp.dot(a, b, preferred_element_type=f32)


def row_of(quantity):
    return GROUP * (quantity // 3) + BASIS * (quantity % 3)


def kernel(n_dom, n_sub, *refs):
    inputs, out_ref, scratch = refs[:13], refs[13], refs[14:]
    held, scratch = scratch[:13], scratch[13:]
    (
        state_ref,
        geometry_ref,
        scale_ref,
        material_ref,
        cluster_ref,
        neighbours_ref,
        orientation_ref,
        stiffness_ref,
        jacobians_ref,
        local_ref,
        neigh_ref,
        plus_ref,
        minus_ref,
    ) = held
    (
        dofs,
        extra,
        small,
        basis,
        fluxes,
        wide,
        right,
        hot,
        table,
        own,
        picked_high,
        picked_low,
        ends,
        packed,
        from_sub,
        from_dom,
        load_sem,
        send_sem,
        recv_sem,
    ) = scratch
    count = state_ref.shape[2]
    dom, sub = lax.axis_index("dom"), lax.axis_index("sub")
    left_dev = (lax.rem(dom + n_dom - 1, n_dom), sub)
    right_dev = (lax.rem(dom + 1, n_dom), sub)
    peers = [(dom, lax.rem(sub + k, n_sub)) for k in range(1, n_sub)]

    barrier = pltpu.get_barrier_semaphore()
    for other in [left_dev, right_dev] + peers:
        pl.semaphore_signal(barrier, inc=1, device_id=other, device_id_type=MESH)
    loads = [pltpu.make_async_copy(inputs[i], held[i], load_sem.at[i]) for i in range(13)]
    for i in (7, 8, 0, 1, 3, 4, 2, 5, 6, 9, 10, 11, 12):
        loads[i].start()

    small[...] = jnp.zeros_like(small)
    fluxes[...] = jnp.zeros_like(fluxes)
    right[...] = jnp.zeros_like(right)
    dofs[...] = jnp.zeros_like(dofs)
    extra[...] = jnp.zeros_like(extra)
    col = iota((16, ROWS), 1)
    _, _, fn, ok = place(col)
    hit = (iota((16, ROWS), 0) == fn) & ok
    pick_high = jnp.where(hit & (col < 2 * GROUP), 1.0, 0.0).astype(bf16)
    pick_low = jnp.where(hit & (col >= 2 * GROUP), 1.0, 0.0).astype(bf16)
    _, third_row, fn_row, ok_row = place(iota((GROUP, ROWS), 0))
    _, third_col, _, ok_col = place(iota((GROUP, ROWS), 1) & (GROUP - 1))
    same_third = (third_row == third_col) & ok_row & ok_col
    _, _, fn, ok = place(iota((GROUP, SLOTS * BASIS), 0))
    offset = jnp.where(ok, iota((GROUP, SLOTS * BASIS), 1) - SLOTS * fn, -1)

    def expand(spread, first, last):
        chosen = [jnp.where(offset == k, 1.0, 0.0).astype(bf16) for k in range(first, last)]
        full = mul(jnp.concatenate(chosen, axis=0), spread)
        for k in range(first, last):
            block = full[GROUP * (k - first) : GROUP * (k - first) + GROUP]
            basis[GROUP * k : GROUP * k + GROUP, :] = jnp.where(same_third, block, 0.0).astype(bf16)

    col = iota((16, 128), 1)
    quantity, _, _, ok = place(col)
    pick = jnp.where((quantity == iota((16, 128), 0)) & ok & (col < ROWS), 1.0, 0.0).astype(bf16)
    _, _, fn_row, ok_row = place(iota((ROWS, 128), 0))
    _, _, fn_col, ok_col = place(iota((ROWS, 128), 1))
    same_fn = (fn_row == fn_col) & ok_row & ok_col & (iota((ROWS, 128), 1) < ROWS)
    quantity, _, _, ok = place(iota((ROWS, 16 * QUANT), 0))
    flux_offset = jnp.where(ok, iota((ROWS, 16 * QUANT), 1) - 16 * quantity, -1)

    def expand_fluxes(slots, blocks):
        high, low = split(fluxes[...].reshape(16 * QUANT, 128)[:, :16])
        spread_high, spread_low = mul(high, pick).astype(bf16), mul(low, pick).astype(bf16)
        spread = jnp.concatenate([spread_high, spread_low], axis=1)
        for m in range(3):
            chosen = [jnp.where(flux_offset == slot[m], 1.0, 0.0).astype(bf16) for slot in slots]
            full = mul(jnp.concatenate(chosen, axis=0), spread)
            for i, (one, two, three) in enumerate(blocks):
                part = full[ROWS * i : ROWS * i + ROWS]
                high = jnp.where(same_fn, part[:, :128], 0.0).astype(bf16)
                low = jnp.where(same_fn, part[:, 128:], 0.0).astype(bf16)
                rows = slice(ROWS * m, ROWS * m + ROWS)
                wide[rows, 128 * one : 128 * one + 128] = high
                wide[rows, 128 * two : 128 * two + 128] = high
                wide[rows, 128 * three : 128 * three + 128] = low

    for i in (7, 8, 0, 1, 3, 4):
        loads[i].wait()
    small[:, :3, :BASIS] = stiffness_ref[...]
    high, low = split(small[...].reshape(SLOTS * BASIS, 128)[:, :16])
    expand((mul(high, pick_high) + mul(low, pick_low)).astype(bf16), 0, 3)

    for m in range(3):
        fluxes[:, 3 * m : 3 * m + 3, :QUANT] = jacobians_ref[m]
    expand_fluxes([(c, 3 + c, 6 + c) for c in range(3)], [(c, 3 + c, 6 + c) for c in range(3)])

    for v in range(QUANT):
        dofs[row_of(v) : row_of(v) + BASIS, :] = state_ref[v]
    material = jnp.broadcast_to(material_ref[...], (ROWS, count))
    coarse = jnp.broadcast_to(cluster_ref[...], (ROWS, count)).astype(f32)

    def on_basis(high, low, first, last):
        parts = []
        for g in range(3):
            h, l = high[GROUP * g : GROUP * g + GROUP], low[GROUP * g : GROUP * g + GROUP]
            parts.append(mul(basis[GROUP * first : GROUP * last, :], jnp.concatenate([h, l, h], axis=0)))
        return [
            jnp.concatenate([part[GROUP * k : GROUP * k + GROUP] for part in parts], axis=0)
            for k in range(last - first)
        ]

    def put(values, blocks, start, length):
        high, low = split(values)
        for block, half in zip(blocks, (high, low, high)):
            right[128 * block + start : 128 * block + start + length, :] = half

    def mixtures(mapped):
        for c in range(3):
            mixture = (
                mapped[0] * geometry_ref[0, c : c + 1, :]
                + mapped[1] * geometry_ref[1, c : c + 1, :]
                + mapped[2] * geometry_ref[2, c : c + 1, :]
            )
            put(mixture, (c, 3 + c, 6 + c), 0, ROWS)

    def on_quantities(first, last):
        every = mul(wide[:, 128 * first : 128 * last], right[128 * first : 128 * last, :])
        return jnp.where(
            material == 0,
            every[:ROWS],
            jnp.where(material == 1, every[ROWS : 2 * ROWS], every[2 * ROWS :]),
        )

    def star(values):
        high, low = split(values)
        mixtures(on_basis(high, low, 0, 3))
        return on_quantities(0, 9)

    def predict(values, shifted):
        first = -star(values)
        second = -star(first)
        values = values + shifted * (step_length * first + 0.5 * step_length**2 * second)
        first = first + shifted * (step_length * second)
        return step_length * values + step_length**2 / 2 * first + step_length**3 / 6 * second

    def halves(values, lanes):
        high, low = split(values)
        table[:ROWS, lanes] = high
        table[ROWS:, lanes] = low

    lane = iota((ROWS // 2, COPY_DEV), 1)
    front = lane < SUB_COPY

    def send(integral, r):
        ends[r, 0] = integral[:, :COPY_DEV]
        ends[r, 1] = integral[:, count - COPY_DEV :]
        top, bottom = integral[: ROWS // 2, :COPY_DEV], integral[ROWS // 2 :, :COPY_DEV]
        mine = jnp.where(front, top, pltpu.roll(bottom, SUB_COPY, 1))
        packed[r] = mine
        from_sub[r, sub] = mine
        copies = []
        for k, (end, other) in enumerate([(1, right_dev), (0, left_dev)]):
            copies.append(
                pltpu.make_async_remote_copy(
                    src_ref=ends.at[r, end],
                    dst_ref=from_dom.at[r, k],
                    send_sem=send_sem.at[r, k],
                    recv_sem=recv_sem.at[r, k],
                    device_id=other,
                    device_id_type=MESH,
                )
            )
        for k, other in enumerate(peers):
            copies.append(
                pltpu.make_async_remote_copy(
                    src_ref=packed.at[r],
                    dst_ref=from_sub.at[r, sub],
                    send_sem=send_sem.at[r, 2 + k],
                    recv_sem=recv_sem.at[r, 2 + k],
                    device_id=other,
                    device_id_type=MESH,
                )
            )
        for copy in copies:
            copy.start()
        return copies

    depth = hot.shape[0]

    def prepare():
        for i in (2, 5, 6, 9, 10, 11, 12):
            loads[i].wait()
        for f in range(4):
            wanted = jnp.broadcast_to(neighbours_ref[f : f + 1, :], (depth, count))
            hit = jnp.where(iota((depth, count), 0) == wanted, 1.0, 0.0)
            hot[:, count * f : count * f + count] = hit.astype(bf16)
        small[:, 6:10, :BASIS] = local_ref[...]
        small[:, 10:22, :BASIS] = neigh_ref[...]
        high, low = split(small[...].reshape(SLOTS * BASIS, 128)[:, :16])
        expand((mul(high, pick_high) + mul(low, pick_low)).astype(bf16), 6, 22)
        which = iota((16, SLOTS * BASIS), 1) - SLOTS * iota((16, SLOTS * BASIS), 0)
        _, _, fn, ok = place(iota((GROUP, 16), 0))
        repeat = jnp.where((fn == iota((GROUP, 16), 1)) & ok, 1.0, 0.0).astype(bf16)
        for k in range(3):
            chosen = jnp.where(which == k, 1.0, 0.0).astype(bf16)
            h, l = mul(chosen, high).T.astype(bf16), mul(chosen, low).T.astype(bf16)
            block = mul(repeat, (mul(h, pick_high) + mul(l, pick_low)).astype(bf16))
            rows = slice(GROUP * (3 + k), GROUP * (4 + k))
            basis[rows, :] = jnp.where(same_third, block, 0.0).astype(bf16)
        fluxes[:, 9:12, :QUANT] = -plus_ref[...]
        fluxes[:, 12:15, :QUANT] = -minus_ref[...]
        expand_fluxes([(9, 10, 11), (12, 13, 14)], [(9, 10, 11), (12, 13, 14)])

    def advance(values, r):
        integral = predict(values, coarse * r.astype(f32))
        pl.when(r == 0)(lambda: pl.semaphore_wait(barrier, n_sub + 1))
        copies = send(integral, r)
        pl.when(r == 0)(prepare)
        high, low = split(integral)
        table[:ROWS, :count] = high
        table[ROWS:, :count] = low
        mapped = on_basis(high, low, 3, 10)
        mixtures(mapped[:3])
        local = mapped[3] * scale_ref[0:1, :]
        for f in range(1, 4):
            local = local + mapped[3 + f] * scale_ref[f : f + 1, :]
        put(local, (9, 10, 11), 0, ROWS)
        change = on_quantities(0, 12)
        for f in range(4):
            lanes = slice(count * f, count * f + count)
            own[:, lanes] = mul(table[:, :count], hot[:count, lanes]).astype(bf16)

        for copy in copies:
            copy.wait()
        for pair in range(n_sub // 2):
            one, two = from_sub[r, 2 * pair], from_sub[r, 2 * pair + 1]
            top = jnp.where(front, one, pltpu.roll(two, SUB_COPY, 1))
            bottom = jnp.where(front, pltpu.roll(one, SUB_COPY, 1), two)
            lanes = slice(count + 128 * pair, count + 128 * pair + 128)
            halves(jnp.concatenate([top, bottom], axis=0), lanes)
        for k in range(2):
            start = count + SUB_COPY * n_sub + COPY_DEV * k
            halves(from_dom[r, k], slice(start, start + COPY_DEV))

        totals = [0.0] * 3
        for f in range(4):
            lanes = slice(count * f, count * f + count)
            found = mul(table[:, count:], hot[count:, lanes]).astype(bf16) + own[:, lanes]
            picked_high[:, lanes] = found[:ROWS]
            picked_low[:, lanes] = found[ROWS:]
            for g in range(3):
                rows = slice(GROUP * g, GROUP * g + GROUP)
                h, l = picked_high[rows, lanes], picked_low[rows, lanes]
                turned = mul(basis[10 * GROUP :, :], jnp.concatenate([h, l, h], axis=0))
                turn = jnp.broadcast_to(orientation_ref[f : f + 1, :], (GROUP, count))
                chosen = turned[:GROUP]
                for t in range(1, 12):
                    chosen = jnp.where(turn == t, turned[GROUP * t : GROUP * t + GROUP], chosen)
                totals[g] = totals[g] + chosen * scale_ref[f : f + 1, :]
        for g in range(3):
            put(totals[g], (12, 13, 14), GROUP * g, GROUP)
        return change + on_quantities(12, 15)

    def half_step(r, carry):
        change = advance(dofs[...], r)
        later = coarse * change
        dofs[...] = dofs[...] + extra[...] + (change - (1 - r).astype(f32) * later)
        extra[...] = later
        return carry

    lax.fori_loop(0, 2, half_step, 0)
    for v in range(QUANT):
        out_ref[v] = dofs[row_of(v) : row_of(v) + BASIS, :]


def shards(n_dom, n_sub, state, geometry, face_scale, material, cluster, neighbours, orientation, *parameters):
    stiffness, jacobians, flux_local, flux_neigh, flux_plus, flux_minus = parameters
    count = state.shape[2]
    depth = count + SUB_COPY * n_sub + 2 * COPY_DEV
    operands = [
        state,
        geometry,
        face_scale,
        material[None],
        cluster[None],
        neighbours,
        orientation,
        stiffness.transpose(1, 0, 2),
        jacobians.transpose(0, 2, 1, 3),
        flux_local.transpose(1, 0, 2),
        flux_neigh.transpose(1, 0, 2),
        flux_plus.transpose(1, 0, 2),
        flux_minus.transpose(1, 0, 2),
    ]
    copies = n_sub + 1
    return pl.pallas_call(
        functools.partial(kernel, n_dom, n_sub),
        out_shape=pltpu.VMEM(state.shape, f32),
        in_specs=[pl.BlockSpec(memory_space=pltpu.HBM)] * 13,
        out_specs=pl.BlockSpec(memory_space=pltpu.VMEM),
        scratch_shapes=[pltpu.VMEM(x.shape, x.dtype) for x in operands]
        + [
            pltpu.VMEM((ROWS, count), f32),
            pltpu.VMEM((ROWS, count), f32),
            pltpu.VMEM((BASIS, SLOTS, 128), f32),
            pltpu.VMEM((22 * GROUP, ROWS), bf16),
            pltpu.VMEM((QUANT, 16, 128), f32),
            pltpu.VMEM((3 * ROWS, 15 * 128), bf16),
            pltpu.VMEM((15 * 128, count), bf16),
            pltpu.VMEM((depth, 4 * count), bf16),
            pltpu.VMEM((2 * ROWS, depth), bf16),
            pltpu.VMEM((2 * ROWS, 4 * count), bf16),
            pltpu.VMEM((ROWS, 4 * count), bf16),
            pltpu.VMEM((ROWS, 4 * count), bf16),
            pltpu.VMEM((2, 2, ROWS, COPY_DEV), f32),
            pltpu.VMEM((2, ROWS // 2, COPY_DEV), f32),
            pltpu.VMEM((2, n_sub, ROWS // 2, COPY_DEV), f32),
            pltpu.VMEM((2, 2, ROWS, COPY_DEV), f32),
            pltpu.SemaphoreType.DMA((13,)),
            pltpu.SemaphoreType.DMA((2, copies)),
            pltpu.SemaphoreType.DMA((2, copies)),
        ],
        compiler_params=pltpu.CompilerParams(
            collective_id=0, has_side_effects=True, vmem_limit_bytes=LIMIT
        ),
    )(*operands)


def solution(mesh):
    placed = (
        P(None, None, ("dom", "sub")),
        P(None, None, ("dom", "sub")),
        P(None, ("dom", "sub")),
        P(("dom", "sub")),
        P(("dom", "sub")),
        P(None, ("dom", "sub")),
        P(None, ("dom", "sub")),
        P(),
        P(),
        P(),
        P(),
        P(),
        P(),
    )
    return jax.shard_map(
        functools.partial(shards, mesh.shape["dom"], mesh.shape["sub"]),
        mesh=mesh,
        in_specs=placed,
        out_specs=P(None, None, ("dom", "sub")),
        check_vma=False,
    )
```

```python
import functools

import jax
import jax.numpy as jnp
from jax import lax
from jax.experimental import pallas as pl
from jax.experimental.pallas import tpu as pltpu
from jax.sharding import PartitionSpec as P

COPY_DEV = 128
SUB_COPY = 64
QUANT = 9
BASIS = 10
GROUP = 32
ROWS = 96
SLOTS = 24
LIMIT = 56 * 1024 * 1024

step_length = 0.2
f32 = jnp.float32
bf16 = jnp.bfloat16
MESH = pl.DeviceIdType.MESH


def iota(shape, dim):
    return lax.broadcasted_iota(jnp.int32, shape, dim)


def place(row):
    inner = row & (GROUP - 1)
    third = (inner >= BASIS).astype(jnp.int32) + (inner >= 2 * BASIS).astype(jnp.int32)
    quantity = 3 * lax.shift_right_logical(row, 5) + third
    return quantity, third, inner - BASIS * third, inner < 3 * BASIS


def split(values):
    high = values.astype(bf16)
    return high, (values - high.astype(f32)).astype(bf16)


def mul(a, b):
    return jnp.dot(a, b, preferred_element_type=f32)


def row_of(quantity):
    return GROUP * (quantity // 3) + BASIS * (quantity % 3)


def kernel(n_dom, n_sub, *refs):
    inputs, out_ref, scratch = refs[:13], refs[13], refs[14:]
    held, scratch = scratch[:13], scratch[13:]
    (
        state_ref,
        geometry_ref,
        scale_ref,
        material_ref,
        cluster_ref,
        neighbours_ref,
        orientation_ref,
        stiffness_ref,
        jacobians_ref,
        local_ref,
        neigh_ref,
        plus_ref,
        minus_ref,
    ) = held
    (
        dofs,
        extra,
        small,
        basis,
        fluxes,
        wide,
        right,
        hot,
        table,
        own,
        picked_high,
        picked_low,
        ends,
        packed,
        from_sub,
        from_dom,
        load_sem,
        send_sem,
        recv_sem,
    ) = scratch
    count = state_ref.shape[2]
    dom, sub = lax.axis_index("dom"), lax.axis_index("sub")
    left_dev = (lax.rem(dom + n_dom - 1, n_dom), sub)
    right_dev = (lax.rem(dom + 1, n_dom), sub)
    peers = [(dom, lax.rem(sub + k, n_sub)) for k in range(1, n_sub)]

    barrier = pltpu.get_barrier_semaphore()
    for other in [left_dev, right_dev] + peers:
        pl.semaphore_signal(barrier, inc=1, device_id=other, device_id_type=MESH)
    loads = [pltpu.make_async_copy(inputs[i], held[i], load_sem.at[i]) for i in range(13)]
    for i in (7, 8, 0, 1, 3, 4, 2, 5, 6, 9, 10, 11, 12):
        loads[i].start()

    small[...] = jnp.zeros_like(small)
    fluxes[...] = jnp.zeros_like(fluxes)
    right[...] = jnp.zeros_like(right)
    dofs[...] = jnp.zeros_like(dofs)
    extra[...] = jnp.zeros_like(extra)
    col = iota((16, ROWS), 1)
    _, _, fn, ok = place(col)
    hit = (iota((16, ROWS), 0) == fn) & ok
    pick_high = jnp.where(hit & (col < 2 * GROUP), 1.0, 0.0).astype(bf16)
    pick_low = jnp.where(hit & (col >= 2 * GROUP), 1.0, 0.0).astype(bf16)
    _, third_row, fn_row, ok_row = place(iota((GROUP, ROWS), 0))
    _, third_col, _, ok_col = place(iota((GROUP, ROWS), 1) & (GROUP - 1))
    same_third = (third_row == third_col) & ok_row & ok_col
    _, _, fn, ok = place(iota((GROUP, SLOTS * BASIS), 0))
    offset = jnp.where(ok, iota((GROUP, SLOTS * BASIS), 1) - SLOTS * fn, -1)

    def expand(spread, first, last):
        chosen = [jnp.where(offset == k, 1.0, 0.0).astype(bf16) for k in range(first, last)]
        full = mul(jnp.concatenate(chosen, axis=0), spread)
        for k in range(first, last):
            block = full[GROUP * (k - first) : GROUP * (k - first) + GROUP]
            basis[GROUP * k : GROUP * k + GROUP, :] = jnp.where(same_third, block, 0.0).astype(bf16)

    col = iota((16, 128), 1)
    quantity, _, _, ok = place(col)
    pick = jnp.where((quantity == iota((16, 128), 0)) & ok & (col < ROWS), 1.0, 0.0).astype(bf16)
    _, _, fn_row, ok_row = place(iota((ROWS, 128), 0))
    _, _, fn_col, ok_col = place(iota((ROWS, 128), 1))
    same_fn = (fn_row == fn_col) & ok_row & ok_col & (iota((ROWS, 128), 1) < ROWS)
    quantity, _, _, ok = place(iota((ROWS, 16 * QUANT), 0))
    flux_offset = jnp.where(ok, iota((ROWS, 16 * QUANT), 1) - 16 * quantity, -1)

    def expand_fluxes(slots, blocks):
        high, low = split(fluxes[...].reshape(16 * QUANT, 128)[:, :16])
        spread_high, spread_low = mul(high, pick).astype(bf16), mul(low, pick).astype(bf16)
        spread = jnp.concatenate([spread_high, spread_low], axis=1)
        for m in range(3):
            chosen = [jnp.where(flux_offset == slot[m], 1.0, 0.0).astype(bf16) for slot in slots]
            full = mul(jnp.concatenate(chosen, axis=0), spread)
            for i, (one, two, three) in enumerate(blocks):
                part = full[ROWS * i : ROWS * i + ROWS]
                high = jnp.where(same_fn, part[:, :128], 0.0).astype(bf16)
                low = jnp.where(same_fn, part[:, 128:], 0.0).astype(bf16)
                rows = slice(ROWS * m, ROWS * m + ROWS)
                wide[rows, 128 * one : 128 * one + 128] = high
                wide[rows, 128 * two : 128 * two + 128] = high
                wide[rows, 128 * three : 128 * three + 128] = low

    for i in (7, 8, 0, 1, 3, 4):
        loads[i].wait()
    small[:, :3, :BASIS] = stiffness_ref[...]
    high, low = split(small[...].reshape(SLOTS * BASIS, 128)[:, :16])
    expand((mul(high, pick_high) + mul(low, pick_low)).astype(bf16), 0, 3)

    for m in range(3):
        fluxes[:, 3 * m : 3 * m + 3, :QUANT] = jacobians_ref[m]
    expand_fluxes([(c, 3 + c, 6 + c) for c in range(3)], [(c, 3 + c, 6 + c) for c in range(3)])

    for v in range(QUANT):
        dofs[row_of(v) : row_of(v) + BASIS, :] = state_ref[v]
    material = jnp.broadcast_to(material_ref[...], (ROWS, count))
    coarse = jnp.broadcast_to(cluster_ref[...], (ROWS, count)).astype(f32)

    def on_basis(high, low, first, last):
        parts = []
        for g in range(3):
            h, l = high[GROUP * g : GROUP * g + GROUP], low[GROUP * g : GROUP * g + GROUP]
            parts.append(mul(basis[GROUP * first : GROUP * last, :], jnp.concatenate([h, l, h], axis=0)))
        return [
            jnp.concatenate([part[GROUP * k : GROUP * k + GROUP] for part in parts], axis=0)
            for k in range(last - first)
        ]

    def put(values, blocks, start, length):
        high, low = split(values)
        for block, half in zip(blocks, (high, low, high)):
            right[128 * block + start : 128 * block + start + length, :] = half

    def mixtures(mapped):
        for c in range(3):
            mixture = (
                mapped[0] * geometry_ref[0, c : c + 1, :]
                + mapped[1] * geometry_ref[1, c : c + 1, :]
                + mapped[2] * geometry_ref[2, c : c + 1, :]
            )
            put(mixture, (c, 3 + c, 6 + c), 0, ROWS)

    def on_quantities(first, last):
        every = mul(wide[:, 128 * first : 128 * last], right[128 * first : 128 * last, :])
        return jnp.where(
            material == 0,
            every[:ROWS],
            jnp.where(material == 1, every[ROWS : 2 * ROWS], every[2 * ROWS :]),
        )

    def star(values):
        high, low = split(values)
        mixtures(on_basis(high, low, 0, 3))
        return on_quantities(0, 9)

    def predict(values, shifted):
        first = -star(values)
        second = -star(first)
        values = values + shifted * (step_length * first + 0.5 * step_length**2 * second)
        first = first + shifted * (step_length * second)
        return step_length * values + step_length**2 / 2 * first + step_length**3 / 6 * second

    def halves(values, lanes):
        high, low = split(values)
        table[:ROWS, lanes] = high
        table[ROWS:, lanes] = low

    lane = iota((ROWS // 2, COPY_DEV), 1)
    front = lane < SUB_COPY

    def send(integral, r):
        ends[r, 0] = integral[:, :COPY_DEV]
        ends[r, 1] = integral[:, count - COPY_DEV :]
        top, bottom = integral[: ROWS // 2, :COPY_DEV], integral[ROWS // 2 :, :COPY_DEV]
        mine = jnp.where(front, top, pltpu.roll(bottom, SUB_COPY, 1))
        packed[r] = mine
        from_sub[r, sub] = mine
        copies = []
        for k, (end, other) in enumerate([(1, right_dev), (0, left_dev)]):
            copies.append(
                pltpu.make_async_remote_copy(
                    src_ref=ends.at[r, end],
                    dst_ref=from_dom.at[r, k],
                    send_sem=send_sem.at[r, k],
                    recv_sem=recv_sem.at[r, k],
                    device_id=other,
                    device_id_type=MESH,
                )
            )
        for k, other in enumerate(peers):
            copies.append(
                pltpu.make_async_remote_copy(
                    src_ref=packed.at[r],
                    dst_ref=from_sub.at[r, sub],
                    send_sem=send_sem.at[r, 2 + k],
                    recv_sem=recv_sem.at[r, 2 + k],
                    device_id=other,
                    device_id_type=MESH,
                )
            )
        for copy in copies:
            copy.start()
        return copies

    depth = hot.shape[0]

    def prepare():
        for i in (2, 5, 6, 9, 10, 11, 12):
            loads[i].wait()
        number = iota((128, count), 0).astype(f32).astype(bf16)
        one, zero = jnp.ones((128, count), bf16), jnp.zeros((128, count), bf16)
        for f in range(4):
            wanted = jnp.broadcast_to(neighbours_ref[f : f + 1, :], (16, count))
            for start in range(0, depth, 128):
                near = jnp.clip(wanted - start, -1, 128).astype(f32).astype(bf16)
                hit = jnp.where(number == jnp.concatenate([near] * 8, axis=0), one, zero)
                hot[start : start + 128, count * f : count * f + count] = hit
        small[:, 6:10, :BASIS] = local_ref[...]
        small[:, 10:22, :BASIS] = neigh_ref[...]
        high, low = split(small[...].reshape(SLOTS * BASIS, 128)[:, :16])
        expand((mul(high, pick_high) + mul(low, pick_low)).astype(bf16), 6, 22)
        which = iota((16, SLOTS * BASIS), 1) - SLOTS * iota((16, SLOTS * BASIS), 0)
        _, _, fn, ok = place(iota((GROUP, 16), 0))
        repeat = jnp.where((fn == iota((GROUP, 16), 1)) & ok, 1.0, 0.0).astype(bf16)
        for k in range(3):
            chosen = jnp.where(which == k, 1.0, 0.0).astype(bf16)
            h, l = mul(chosen, high).T.astype(bf16), mul(chosen, low).T.astype(bf16)
            block = mul(repeat, (mul(h, pick_high) + mul(l, pick_low)).astype(bf16))
            rows = slice(GROUP * (3 + k), GROUP * (4 + k))
            basis[rows, :] = jnp.where(same_third, block, 0.0).astype(bf16)
        fluxes[:, 9:12, :QUANT] = -plus_ref[...]
        fluxes[:, 12:15, :QUANT] = -minus_ref[...]
        expand_fluxes([(9, 10, 11), (12, 13, 14)], [(9, 10, 11), (12, 13, 14)])

    def advance(values, r):
        integral = predict(values, coarse * r.astype(f32))
        pl.when(r == 0)(lambda: pl.semaphore_wait(barrier, n_sub + 1))
        copies = send(integral, r)
        pl.when(r == 0)(prepare)
        high, low = split(integral)
        table[:ROWS, :count] = high
        table[ROWS:, :count] = low
        mapped = on_basis(high, low, 3, 10)
        mixtures(mapped[:3])
        local = mapped[3] * scale_ref[0:1, :]
        for f in range(1, 4):
            local = local + mapped[3 + f] * scale_ref[f : f + 1, :]
        put(local, (9, 10, 11), 0, ROWS)
        change = on_quantities(0, 12)

        for copy in copies[2:]:
            copy.wait()
        near = count + SUB_COPY * n_sub
        for pair in range(n_sub // 2):
            one, two = from_sub[r, 2 * pair], from_sub[r, 2 * pair + 1]
            top = jnp.where(front, one, pltpu.roll(two, SUB_COPY, 1))
            bottom = jnp.where(front, pltpu.roll(one, SUB_COPY, 1), two)
            lanes = slice(count + 128 * pair, count + 128 * pair + 128)
            halves(jnp.concatenate([top, bottom], axis=0), lanes)
        for f in range(4):
            lanes = slice(count * f, count * f + count)
            own[:, lanes] = mul(table[:, :near], hot[:near, lanes]).astype(bf16)

        for copy in copies[:2]:
            copy.wait()
        for k in range(2):
            halves(from_dom[r, k], slice(near + COPY_DEV * k, near + COPY_DEV * (k + 1)))

        totals = [0.0] * 3
        for f in range(4):
            lanes = slice(count * f, count * f + count)
            found = mul(table[:, near:], hot[near:, lanes]).astype(bf16) + own[:, lanes]
            picked_high[:, lanes] = found[:ROWS]
            picked_low[:, lanes] = found[ROWS:]
            for g in range(3):
                rows = slice(GROUP * g, GROUP * g + GROUP)
                h, l = picked_high[rows, lanes], picked_low[rows, lanes]
                turned = mul(basis[10 * GROUP :, :], jnp.concatenate([h, l, h], axis=0))
                turn = jnp.broadcast_to(orientation_ref[f : f + 1, :], (GROUP, count))
                chosen = turned[:GROUP]
                for t in range(1, 12):
                    chosen = jnp.where(turn == t, turned[GROUP * t : GROUP * t + GROUP], chosen)
                totals[g] = totals[g] + chosen * scale_ref[f : f + 1, :]
        for g in range(3):
            put(totals[g], (12, 13, 14), GROUP * g, GROUP)
        return change + on_quantities(12, 15)

    def half_step(r, carry):
        change = advance(dofs[...], r)
        later = coarse * change
        dofs[...] = dofs[...] + extra[...] + (change - (1 - r).astype(f32) * later)
        extra[...] = later
        return carry

    lax.fori_loop(0, 2, half_step, 0)
    for v in range(QUANT):
        out_ref[v] = dofs[row_of(v) : row_of(v) + BASIS, :]


def shards(n_dom, n_sub, state, geometry, face_scale, material, cluster, neighbours, orientation, *parameters):
    stiffness, jacobians, flux_local, flux_neigh, flux_plus, flux_minus = parameters
    count = state.shape[2]
    depth = count + SUB_COPY * n_sub + 2 * COPY_DEV
    operands = [
        state,
        geometry,
        face_scale,
        material[None],
        cluster[None],
        neighbours,
        orientation,
        stiffness.transpose(1, 0, 2),
        jacobians.transpose(0, 2, 1, 3),
        flux_local.transpose(1, 0, 2),
        flux_neigh.transpose(1, 0, 2),
        flux_plus.transpose(1, 0, 2),
        flux_minus.transpose(1, 0, 2),
    ]
    copies = n_sub + 1
    return pl.pallas_call(
        functools.partial(kernel, n_dom, n_sub),
        out_shape=pltpu.VMEM(state.shape, f32),
        in_specs=[pl.BlockSpec(memory_space=pltpu.HBM)] * 13,
        out_specs=pl.BlockSpec(memory_space=pltpu.VMEM),
        scratch_shapes=[pltpu.VMEM(x.shape, x.dtype) for x in operands]
        + [
            pltpu.VMEM((ROWS, count), f32),
            pltpu.VMEM((ROWS, count), f32),
            pltpu.VMEM((BASIS, SLOTS, 128), f32),
            pltpu.VMEM((22 * GROUP, ROWS), bf16),
            pltpu.VMEM((QUANT, 16, 128), f32),
            pltpu.VMEM((3 * ROWS, 15 * 128), bf16),
            pltpu.VMEM((15 * 128, count), bf16),
            pltpu.VMEM((depth, 4 * count), bf16),
            pltpu.VMEM((2 * ROWS, depth), bf16),
            pltpu.VMEM((2 * ROWS, 4 * count), bf16),
            pltpu.VMEM((ROWS, 4 * count), bf16),
            pltpu.VMEM((ROWS, 4 * count), bf16),
            pltpu.VMEM((2, 2, ROWS, COPY_DEV), f32),
            pltpu.VMEM((2, ROWS // 2, COPY_DEV), f32),
            pltpu.VMEM((2, n_sub, ROWS // 2, COPY_DEV), f32),
            pltpu.VMEM((2, 2, ROWS, COPY_DEV), f32),
            pltpu.SemaphoreType.DMA((13,)),
            pltpu.SemaphoreType.DMA((2, copies)),
            pltpu.SemaphoreType.DMA((2, copies)),
        ],
        compiler_params=pltpu.CompilerParams(
            collective_id=0, has_side_effects=True, vmem_limit_bytes=LIMIT
        ),
    )(*operands)


def solution(mesh):
    placed = (
        P(None, None, ("dom", "sub")),
        P(None, None, ("dom", "sub")),
        P(None, ("dom", "sub")),
        P(("dom", "sub")),
        P(("dom", "sub")),
        P(None, ("dom", "sub")),
        P(None, ("dom", "sub")),
        P(),
        P(),
        P(),
        P(),
        P(),
        P(),
    )
    return jax.shard_map(
        functools.partial(shards, mesh.shape["dom"], mesh.shape["sub"]),
        mesh=mesh,
        in_specs=placed,
        out_specs=P(None, None, ("dom", "sub")),
        check_vma=False,
    )
```

```python
import functools

import jax
import jax.numpy as jnp
from jax import lax
from jax.experimental import pallas as pl
from jax.experimental.pallas import tpu as pltpu
from jax.sharding import PartitionSpec as P

COPY_DEV = 128
SUB_COPY = 64
QUANT = 9
BASIS = 10
GROUP = 32
ROWS = 96
SLOTS = 24
LIMIT = 56 * 1024 * 1024

step_length = 0.2
f32 = jnp.float32
bf16 = jnp.bfloat16
MESH = pl.DeviceIdType.MESH


def iota(shape, dim):
    return lax.broadcasted_iota(jnp.int32, shape, dim)


def place(row):
    inner = row & (GROUP - 1)
    third = (inner >= BASIS).astype(jnp.int32) + (inner >= 2 * BASIS).astype(jnp.int32)
    quantity = 3 * lax.shift_right_logical(row, 5) + third
    return quantity, third, inner - BASIS * third, inner < 3 * BASIS


def split(values):
    high = values.astype(bf16)
    return high, (values - high.astype(f32)).astype(bf16)


def mul(a, b):
    return jnp.dot(a, b, preferred_element_type=f32)


def row_of(quantity):
    return GROUP * (quantity // 3) + BASIS * (quantity % 3)


def kernel(n_dom, n_sub, *refs):
    inputs, out_ref, scratch = refs[:13], refs[13], refs[14:]
    held, scratch = scratch[:13], scratch[13:]
    (
        state_ref,
        geometry_ref,
        scale_ref,
        material_ref,
        cluster_ref,
        neighbours_ref,
        orientation_ref,
        stiffness_ref,
        jacobians_ref,
        local_ref,
        neigh_ref,
        plus_ref,
        minus_ref,
    ) = held
    (
        dofs,
        small,
        basis,
        fluxes,
        wide,
        right,
        hot,
        table,
        own,
        picked_high,
        picked_low,
        ends,
        packed,
        from_sub,
        from_dom,
        load_sem,
        send_sem,
        recv_sem,
    ) = scratch
    count = state_ref.shape[2]
    dom, sub = lax.axis_index("dom"), lax.axis_index("sub")
    left_dev = (lax.rem(dom + n_dom - 1, n_dom), sub)
    right_dev = (lax.rem(dom + 1, n_dom), sub)
    peers = [(dom, lax.rem(sub + k, n_sub)) for k in range(1, n_sub)]

    barrier = pltpu.get_barrier_semaphore()
    for other in [left_dev, right_dev] + peers:
        pl.semaphore_signal(barrier, inc=1, device_id=other, device_id_type=MESH)
    loads = [pltpu.make_async_copy(inputs[i], held[i], load_sem.at[i]) for i in range(13)]
    for i in (7, 8, 0, 1, 3, 4, 2, 5, 6, 9, 10, 11, 12):
        loads[i].start()

    small[...] = jnp.zeros_like(small)
    fluxes[...] = jnp.zeros_like(fluxes)
    right[...] = jnp.zeros_like(right)
    dofs[...] = jnp.zeros_like(dofs)
    col = iota((16, ROWS), 1)
    _, _, fn, ok = place(col)
    hit = (iota((16, ROWS), 0) == fn) & ok
    pick_high = jnp.where(hit & (col < 2 * GROUP), 1.0, 0.0).astype(bf16)
    pick_low = jnp.where(hit & (col >= 2 * GROUP), 1.0, 0.0).astype(bf16)
    _, third_row, fn_row, ok_row = place(iota((GROUP, ROWS), 0))
    _, third_col, _, ok_col = place(iota((GROUP, ROWS), 1) & (GROUP - 1))
    same_third = (third_row == third_col) & ok_row & ok_col
    _, _, fn, ok = place(iota((GROUP, SLOTS * BASIS), 0))
    offset = jnp.where(ok, iota((GROUP, SLOTS * BASIS), 1) - SLOTS * fn, -1)

    def expand(spread, first, last):
        chosen = [jnp.where(offset == k, 1.0, 0.0).astype(bf16) for k in range(first, last)]
        full = mul(jnp.concatenate(chosen, axis=0), spread)
        for k in range(first, last):
            block = full[GROUP * (k - first) : GROUP * (k - first) + GROUP]
            basis[GROUP * k : GROUP * k + GROUP, :] = jnp.where(same_third, block, 0.0).astype(bf16)

    col = iota((16, 128), 1)
    quantity, _, _, ok = place(col)
    pick = jnp.where((quantity == iota((16, 128), 0)) & ok & (col < ROWS), 1.0, 0.0).astype(bf16)
    _, _, fn_row, ok_row = place(iota((ROWS, 128), 0))
    _, _, fn_col, ok_col = place(iota((ROWS, 128), 1))
    same_fn = (fn_row == fn_col) & ok_row & ok_col & (iota((ROWS, 128), 1) < ROWS)
    quantity, _, _, ok = place(iota((ROWS, 16 * QUANT), 0))
    flux_offset = jnp.where(ok, iota((ROWS, 16 * QUANT), 1) - 16 * quantity, -1)

    def expand_fluxes(slots, blocks):
        high, low = split(fluxes[...].reshape(16 * QUANT, 128)[:, :16])
        spread_high, spread_low = mul(high, pick).astype(bf16), mul(low, pick).astype(bf16)
        spread = jnp.concatenate([spread_high, spread_low], axis=1)
        for m in range(3):
            chosen = [jnp.where(flux_offset == slot[m], 1.0, 0.0).astype(bf16) for slot in slots]
            full = mul(jnp.concatenate(chosen, axis=0), spread)
            for i, (one, two, three) in enumerate(blocks):
                part = full[ROWS * i : ROWS * i + ROWS]
                high = jnp.where(same_fn, part[:, :128], 0.0).astype(bf16)
                low = jnp.where(same_fn, part[:, 128:], 0.0).astype(bf16)
                rows = slice(ROWS * m, ROWS * m + ROWS)
                wide[rows, 128 * one : 128 * one + 128] = high
                wide[rows, 128 * two : 128 * two + 128] = high
                wide[rows, 128 * three : 128 * three + 128] = low

    for i in (7, 8, 0, 1, 3, 4):
        loads[i].wait()
    small[:, :3, :BASIS] = stiffness_ref[...]
    high, low = split(small[...].reshape(SLOTS * BASIS, 128)[:, :16])
    expand((mul(high, pick_high) + mul(low, pick_low)).astype(bf16), 0, 3)

    for m in range(3):
        fluxes[:, 3 * m : 3 * m + 3, :QUANT] = jacobians_ref[m]
    expand_fluxes([(c, 3 + c, 6 + c) for c in range(3)], [(c, 3 + c, 6 + c) for c in range(3)])

    for v in range(QUANT):
        dofs[row_of(v) : row_of(v) + BASIS, :] = state_ref[v]
    material = jnp.broadcast_to(material_ref[...], (ROWS, count))
    coarse = jnp.broadcast_to(cluster_ref[...], (ROWS, count)).astype(f32)

    def on_basis(high, low, first, last):
        parts = []
        for g in range(3):
            h, l = high[GROUP * g : GROUP * g + GROUP], low[GROUP * g : GROUP * g + GROUP]
            parts.append(mul(basis[GROUP * first : GROUP * last, :], jnp.concatenate([h, l, h], axis=0)))
        return [
            jnp.concatenate([part[GROUP * k : GROUP * k + GROUP] for part in parts], axis=0)
            for k in range(last - first)
        ]

    def put(values, blocks, start, length):
        high, low = split(values)
        for block, half in zip(blocks, (high, low, high)):
            right[128 * block + start : 128 * block + start + length, :] = half

    def mixtures(mapped):
        for c in range(3):
            mixture = (
                mapped[0] * geometry_ref[0, c : c + 1, :]
                + mapped[1] * geometry_ref[1, c : c + 1, :]
                + mapped[2] * geometry_ref[2, c : c + 1, :]
            )
            put(mixture, (c, 3 + c, 6 + c), 0, ROWS)

    def on_quantities(first, last):
        every = mul(wide[:, 128 * first : 128 * last], right[128 * first : 128 * last, :])
        return jnp.where(
            material == 0,
            every[:ROWS],
            jnp.where(material == 1, every[ROWS : 2 * ROWS], every[2 * ROWS :]),
        )

    def star(values):
        high, low = split(values)
        mixtures(on_basis(high, low, 0, 3))
        return on_quantities(0, 9)

    def predict(values, shifted):
        first = -star(values)
        second = -star(first)
        if shifted:
            values = values + coarse * (step_length * first + 0.5 * step_length**2 * second)
            first = first + coarse * (step_length * second)
        return step_length * values + step_length**2 / 2 * first + step_length**3 / 6 * second

    def halves(values, lanes):
        high, low = split(values)
        table[:ROWS, lanes] = high
        table[ROWS:, lanes] = low

    lane = iota((ROWS // 2, COPY_DEV), 1)
    front = lane < SUB_COPY

    def send(integral, r):
        ends[r, 0] = integral[:, :COPY_DEV]
        ends[r, 1] = integral[:, count - COPY_DEV :]
        top, bottom = integral[: ROWS // 2, :COPY_DEV], integral[ROWS // 2 :, :COPY_DEV]
        mine = jnp.where(front, top, pltpu.roll(bottom, SUB_COPY, 1))
        packed[r] = mine
        from_sub[r, sub] = mine
        copies = []
        for k, (end, other) in enumerate([(1, right_dev), (0, left_dev)]):
            copies.append(
                pltpu.make_async_remote_copy(
                    src_ref=ends.at[r, end],
                    dst_ref=from_dom.at[r, k],
                    send_sem=send_sem.at[r, k],
                    recv_sem=recv_sem.at[r, k],
                    device_id=other,
                    device_id_type=MESH,
                )
            )
        for k, other in enumerate(peers):
            copies.append(
                pltpu.make_async_remote_copy(
                    src_ref=packed.at[r],
                    dst_ref=from_sub.at[r, sub],
                    send_sem=send_sem.at[r, 2 + k],
                    recv_sem=recv_sem.at[r, 2 + k],
                    device_id=other,
                    device_id_type=MESH,
                )
            )
        for copy in copies:
            copy.start()
        return copies

    depth = hot.shape[0]

    def prepare():
        for i in (2, 5, 6, 9, 10, 11, 12):
            loads[i].wait()
        number = iota((128, count), 0).astype(f32).astype(bf16)
        one, zero = jnp.ones((128, count), bf16), jnp.zeros((128, count), bf16)
        for f in range(4):
            wanted = jnp.broadcast_to(neighbours_ref[f : f + 1, :], (16, count))
            for start in range(0, depth, 128):
                near = jnp.clip(wanted - start, -1, 128).astype(f32).astype(bf16)
                hit = jnp.where(number == jnp.concatenate([near] * 8, axis=0), one, zero)
                hot[start : start + 128, count * f : count * f + count] = hit
        small[:, 6:10, :BASIS] = local_ref[...]
        small[:, 10:22, :BASIS] = neigh_ref[...]
        high, low = split(small[...].reshape(SLOTS * BASIS, 128)[:, :16])
        expand((mul(high, pick_high) + mul(low, pick_low)).astype(bf16), 6, 22)
        which = iota((16, SLOTS * BASIS), 1) - SLOTS * iota((16, SLOTS * BASIS), 0)
        _, _, fn, ok = place(iota((GROUP, 16), 0))
        repeat = jnp.where((fn == iota((GROUP, 16), 1)) & ok, 1.0, 0.0).astype(bf16)
        for k in range(3):
            chosen = jnp.where(which == k, 1.0, 0.0).astype(bf16)
            h, l = mul(chosen, high).T.astype(bf16), mul(chosen, low).T.astype(bf16)
            block = mul(repeat, (mul(h, pick_high) + mul(l, pick_low)).astype(bf16))
            rows = slice(GROUP * (3 + k), GROUP * (4 + k))
            basis[rows, :] = jnp.where(same_third, block, 0.0).astype(bf16)
        fluxes[:, 9:12, :QUANT] = -plus_ref[...]
        fluxes[:, 12:15, :QUANT] = -minus_ref[...]
        expand_fluxes([(9, 10, 11), (12, 13, 14)], [(9, 10, 11), (12, 13, 14)])

    def advance(values, r):
        integral = predict(values, r == 1)
        if r == 0:
            pl.semaphore_wait(barrier, n_sub + 1)
        copies = send(integral, r)
        if r == 0:
            prepare()
        high, low = split(integral)
        table[:ROWS, :count] = high
        table[ROWS:, :count] = low
        mapped = on_basis(high, low, 3, 10)
        mixtures(mapped[:3])
        local = mapped[3] * scale_ref[0:1, :]
        for f in range(1, 4):
            local = local + mapped[3 + f] * scale_ref[f : f + 1, :]
        put(local, (9, 10, 11), 0, ROWS)
        change = on_quantities(0, 12)

        for copy in copies[2:]:
            copy.wait()
        near = count + SUB_COPY * n_sub
        for pair in range(n_sub // 2):
            one, two = from_sub[r, 2 * pair], from_sub[r, 2 * pair + 1]
            top = jnp.where(front, one, pltpu.roll(two, SUB_COPY, 1))
            bottom = jnp.where(front, pltpu.roll(one, SUB_COPY, 1), two)
            lanes = slice(count + 128 * pair, count + 128 * pair + 128)
            halves(jnp.concatenate([top, bottom], axis=0), lanes)
        for f in range(4):
            lanes = slice(count * f, count * f + count)
            own[:, lanes] = mul(table[:, :near], hot[:near, lanes]).astype(bf16)

        for copy in copies[:2]:
            copy.wait()
        for k in range(2):
            halves(from_dom[r, k], slice(near + COPY_DEV * k, near + COPY_DEV * (k + 1)))

        totals = [0.0] * 3
        for f in range(4):
            lanes = slice(count * f, count * f + count)
            found = mul(table[:, near:], hot[near:, lanes]).astype(bf16) + own[:, lanes]
            picked_high[:, lanes] = found[:ROWS]
            picked_low[:, lanes] = found[ROWS:]
            for g in range(3):
                rows = slice(GROUP * g, GROUP * g + GROUP)
                h, l = picked_high[rows, lanes], picked_low[rows, lanes]
                turned = mul(basis[10 * GROUP :, :], jnp.concatenate([h, l, h], axis=0))
                turn = jnp.broadcast_to(orientation_ref[f : f + 1, :], (GROUP, count))
                chosen = turned[:GROUP]
                for t in range(1, 12):
                    chosen = jnp.where(turn == t, turned[GROUP * t : GROUP * t + GROUP], chosen)
                totals[g] = totals[g] + chosen * scale_ref[f : f + 1, :]
        for g in range(3):
            put(totals[g], (12, 13, 14), GROUP * g, GROUP)
        return change + on_quantities(12, 15)

    state = dofs[...]
    first_change = advance(state, 0)
    middle = state + (1.0 - coarse) * first_change
    second_change = advance(middle, 1)
    dofs[...] = middle + second_change + coarse * first_change
    for v in range(QUANT):
        out_ref[v] = dofs[row_of(v) : row_of(v) + BASIS, :]


def shards(n_dom, n_sub, state, geometry, face_scale, material, cluster, neighbours, orientation, *parameters):
    stiffness, jacobians, flux_local, flux_neigh, flux_plus, flux_minus = parameters
    count = state.shape[2]
    depth = count + SUB_COPY * n_sub + 2 * COPY_DEV
    operands = [
        state,
        geometry,
        face_scale,
        material[None],
        cluster[None],
        neighbours,
        orientation,
        stiffness.transpose(1, 0, 2),
        jacobians.transpose(0, 2, 1, 3),
        flux_local.transpose(1, 0, 2),
        flux_neigh.transpose(1, 0, 2),
        flux_plus.transpose(1, 0, 2),
        flux_minus.transpose(1, 0, 2),
    ]
    copies = n_sub + 1
    return pl.pallas_call(
        functools.partial(kernel, n_dom, n_sub),
        out_shape=pltpu.VMEM(state.shape, f32),
        in_specs=[pl.BlockSpec(memory_space=pltpu.HBM)] * 13,
        out_specs=pl.BlockSpec(memory_space=pltpu.VMEM),
        scratch_shapes=[pltpu.VMEM(x.shape, x.dtype) for x in operands]
        + [
            pltpu.VMEM((ROWS, count), f32),
            pltpu.VMEM((BASIS, SLOTS, 128), f32),
            pltpu.VMEM((22 * GROUP, ROWS), bf16),
            pltpu.VMEM((QUANT, 16, 128), f32),
            pltpu.VMEM((3 * ROWS, 15 * 128), bf16),
            pltpu.VMEM((15 * 128, count), bf16),
            pltpu.VMEM((depth, 4 * count), bf16),
            pltpu.VMEM((2 * ROWS, depth), bf16),
            pltpu.VMEM((2 * ROWS, 4 * count), bf16),
            pltpu.VMEM((ROWS, 4 * count), bf16),
            pltpu.VMEM((ROWS, 4 * count), bf16),
            pltpu.VMEM((2, 2, ROWS, COPY_DEV), f32),
            pltpu.VMEM((2, ROWS // 2, COPY_DEV), f32),
            pltpu.VMEM((2, n_sub, ROWS // 2, COPY_DEV), f32),
            pltpu.VMEM((2, 2, ROWS, COPY_DEV), f32),
            pltpu.SemaphoreType.DMA((13,)),
            pltpu.SemaphoreType.DMA((2, copies)),
            pltpu.SemaphoreType.DMA((2, copies)),
        ],
        compiler_params=pltpu.CompilerParams(
            collective_id=0, has_side_effects=True, vmem_limit_bytes=LIMIT
        ),
    )(*operands)


def solution(mesh):
    placed = (
        P(None, None, ("dom", "sub")),
        P(None, None, ("dom", "sub")),
        P(None, ("dom", "sub")),
        P(("dom", "sub")),
        P(("dom", "sub")),
        P(None, ("dom", "sub")),
        P(None, ("dom", "sub")),
        P(),
        P(),
        P(),
        P(),
        P(),
        P(),
    )
    return jax.shard_map(
        functools.partial(shards, mesh.shape["dom"], mesh.shape["sub"]),
        mesh=mesh,
        in_specs=placed,
        out_specs=P(None, None, ("dom", "sub")),
        check_vma=False,
    )
```
